32 devices in a mesh: doc: 4 (over z), ctx: 8 (over y, x, core).
Axes of the slice: x: 2, y: 2, z: 4, core: 2. Of those that a mesh axis runs over, the one named last changes fastest.
Arguments:
- queries: bfloat16 [4, 1024, 4096], P('doc', 'ctx'), may hold values from -6 to 6
- out_grad: bfloat16 [4, 1024, 4096], P('doc', 'ctx'), may hold values from -6 to 6
- mem_keys: bfloat16 [4, 64, 4096], P('doc', 'ctx'), may hold values from -6 to 6
- mem_values: bfloat16 [4, 64, 4096], P('doc', 'ctx'), may hold values from -6 to 6
Outputs:
- grad_queries: float32 [4, 1024, 4096], P('doc', 'ctx')
- grad_keys: float32 [4, 64, 4096], P('doc', 'ctx')
- grad_values: float32 [4, 64, 4096], P('doc', 'ctx')
The draws below stay inside these ranges and needn't reach their ends.
All inputs are finite; a program needn't handle non-finite values.
Results may differ from the reference program's by a relative error of at most 0.0011.
Values may be sent and summed in bfloat16 or wider, within the bound.
A program may use at most 64 MiB of HBM per device.

```python
import math
import jax
import jax.numpy as jnp
from jax import lax

HEADS = 32
HD = 128
MEM = 64
QLEN = 1024
DOCS = 4


def draw_mem_keys(key, part):
    first, second = jax.random.split(key, 2)
    row_scale = jnp.exp(jax.random.uniform(second, (DOCS, MEM, HEADS, 1), jnp.float32, math.log(0.25), math.log(2.5)))
    doc_scale = 0.7 + 0.6 * jnp.arange(DOCS, dtype=jnp.float32) / max(DOCS - 1, 1)
    doc_scale = doc_scale.reshape(DOCS, 1, 1, 1)
    base = jax.random.truncated_normal(first, -4.0, 4.0, (DOCS, MEM, HEADS, HD), jnp.float32)
    return (0.4 * base * row_scale * doc_scale).reshape(DOCS, MEM, HEADS * HD).astype(jnp.bfloat16)


def block_scale(rng, extent, cuts, low, top_value):
    gain = 1.0
    for position, parts in cuts:
        heights = jax.random.uniform(jax.random.fold_in(jax.random.fold_in(rng, 6), position), (parts,), jnp.float32, low / len(cuts), top_value / len(cuts))
        gain = gain * jnp.repeat(jnp.exp(heights), extent[position] // parts).reshape((-1,) + (1,) * (len(extent) - 1 - position))
    return gain


def bell_draw(own_key, shape, width, most, shards=(), kind=jnp.bfloat16):
    loudness = block_scale(own_key, shape, shards, -0.22, 0.18) if shards else 1.0
    values = jax.random.normal(own_key, shape, jnp.float32) * width * loudness
    return jnp.minimum(jnp.maximum(values, -most), most).astype(kind)


def setup_inputs(seed: int = 0) -> dict:
    keys = jax.random.split(jax.random.key(seed), 5)
    queries = bell_draw(keys[0], (DOCS, QLEN, HEADS * HD), 1.0, 6.0, ((0, 4), (1, 8)))
    out_grad = bell_draw(keys[1], (DOCS, QLEN, HEADS * HD), 1.0, 6.0, ((0, 4), (1, 8)))
    mem_keys = draw_mem_keys(jax.random.fold_in(keys[4], 71), 0)
    mem_values = bell_draw(keys[3], (DOCS, MEM, HEADS * HD), 1.0, 6.0, ((0, 4), (1, 8)))
    return dict(queries=queries, out_grad=out_grad, mem_keys=mem_keys, mem_values=mem_values)


def reference(queries, out_grad, mem_keys, mem_values):
    scale = HD ** -0.5
    high = lax.Precision.HIGHEST

    def split(x):
        return jnp.transpose(x.astype(jnp.float32).reshape(-1, HEADS, HD), (1, 0, 2))

    def one_head(items):
        q_rows, g_rows, k_rows, v_rows = items
        expo = jnp.exp(jnp.dot(q_rows, k_rows.T, precision=high) * scale)
        dprob = jnp.dot(g_rows, v_rows.T, precision=high)
        norm = jnp.sum(expo, axis=1, keepdims=True)
        drift = jnp.sum(expo * dprob, axis=1, keepdims=True) / norm
        prob = expo / norm
        dscore = prob * (dprob - drift)
        grad_q = jnp.dot(dscore, k_rows, precision=high) * scale
        grad_k = jnp.dot(dscore.T, q_rows, precision=high) * scale
        grad_v = jnp.dot(prob.T, g_rows, precision=high)
        return grad_q, grad_k, grad_v

    grad_q, grad_k, grad_v = lax.map(one_head, (split(queries), split(out_grad), split(mem_keys), split(mem_values)))

    def join(x, rows):
        return jnp.transpose(x, (1, 0, 2)).reshape(DOCS, rows, HEADS * HD)

    return join(grad_q, QLEN), join(grad_k, MEM), join(grad_v, MEM)
```

```python
import functools

import jax
import jax.numpy as jnp
from jax import lax
from jax.experimental import pallas as pl
from jax.experimental.pallas import tpu as pltpu
from jax.sharding import PartitionSpec as P

HD = 128
MESH = pl.DeviceIdType.MESH
NT = (((1,), (1,)), ((), ()))
NN = (((1,), (0,)), ((), ()))
TN = (((0,), (0,)), ((), ()))


def dot(a, b, dims):
    return lax.dot_general(a, b, dims, preferred_element_type=jnp.float32)


def partner(me, step, n):
    if n & (n - 1):
        return lax.rem(me + step, n)
    out, bit = 0, 1
    while bit < n:
        out = out + ((me // bit + step // bit) % 2) * bit
        bit *= 2
    return out


def source(me, step, n):
    if n & (n - 1):
        return lax.rem(me - step + n, n)
    return partner(me, step, n)


def split16(x):
    high = x.astype(jnp.bfloat16)
    return high, (x - high.astype(jnp.float32)).astype(jnp.bfloat16)


def kernel(
    n, ndoc, rows, rows_p,
    q_ref, g_ref, kv_ref,
    gq_out, gk_out, gv_out,
    qbuf, gbuf, kvbuf, keys, values, gqbuf, acc, rsbuf, fin_src, fin,
    kvs, kvr, qs, qr, gs, gr, zs, zr, os, orr, rs, rr, fs, fr,
):
    c = lax.axis_index("ctx")
    d = lax.axis_index("doc")
    width = qbuf.shape[2]
    nheads = width // HD
    total = ndoc * n * rows_p

    def cols(i):
        return pl.ds(pl.multiple_of(i * width, width), width)

    barrier = pltpu.get_barrier_semaphore()

    @pl.loop(1, n)
    def _(s):
        pl.semaphore_signal(barrier, inc=1, device_id=(d, lax.rem(c + s, n)), device_id_type=MESH)

    @pl.loop(1, ndoc)
    def _(t):
        pl.semaphore_signal(barrier, inc=1, device_id=(lax.rem(d + t, ndoc), c), device_id_type=MESH)

    pl.semaphore_wait(barrier, n - 1 + ndoc - 1)

    def kv_send(p):
        return pltpu.make_async_remote_copy(
            src_ref=kv_ref.at[:, cols(p)], dst_ref=kvbuf.at[d * n + c],
            send_sem=kvs.at[p], recv_sem=kvr.at[c], device_id=(d, p), device_id_type=MESH)

    def q_send(p):
        return pltpu.make_async_remote_copy(
            src_ref=q_ref.at[:, cols(p)], dst_ref=qbuf.at[c],
            send_sem=qs.at[p], recv_sem=qr.at[c], device_id=(d, p), device_id_type=MESH)

    def g_send(p):
        return pltpu.make_async_remote_copy(
            src_ref=g_ref.at[:, cols(p)], dst_ref=gbuf.at[c],
            send_sem=gs.at[p], recv_sem=gr.at[c], device_id=(d, p), device_id_type=MESH)

    def z_send(t):
        return pltpu.make_async_remote_copy(
            src_ref=kvbuf.at[pl.ds(d * n, n)], dst_ref=kvbuf.at[pl.ds(d * n, n)],
            send_sem=zs.at[t], recv_sem=zr.at[t],
            device_id=(lax.rem(d + t, ndoc), c), device_id_type=MESH)

    def o_send(p):
        return pltpu.make_async_remote_copy(
            src_ref=gqbuf.at[p], dst_ref=gq_out.at[:, cols(c)],
            send_sem=os.at[p], recv_sem=orr.at[c], device_id=(d, p), device_id_type=MESH)

    def r_send(t):
        to = lax.rem(d + t, ndoc)
        return pltpu.make_async_remote_copy(
            src_ref=acc.at[pl.ds(to * n, n)], dst_ref=rsbuf.at[t],
            send_sem=rs.at[t], recv_sem=rr.at[t], device_id=(to, c), device_id_type=MESH)

    def f_send(p):
        return pltpu.make_async_remote_copy(
            src_ref=fin_src.at[p], dst_ref=fin.at[c],
            send_sem=fs.at[p], recv_sem=fr.at[c], device_id=(d, p), device_id_type=MESH)

    kv_own = pltpu.make_async_copy(kv_ref.at[:, cols(c)], kvbuf.at[d * n + c], kvr.at[c])
    q_own = pltpu.make_async_copy(q_ref.at[:, cols(c)], qbuf.at[c], qr.at[c])
    g_own = pltpu.make_async_copy(g_ref.at[:, cols(c)], gbuf.at[c], gr.at[c])
    kv_own.start()

    @pl.loop(1, n)
    def _(s):
        kv_send(partner(c, s, n)).start()

    q_own.start()
    g_own.start()

    @pl.loop(1, n)
    def _(s):
        p = partner(c, s, n)
        q_send(p).start()
        g_send(p).start()

    @pl.loop(0, n)
    def _(i):
        slab = kvbuf.at[d * n + i]
        pltpu.make_async_copy(slab, slab, kvr.at[i]).wait()

    @pl.loop(1, ndoc)
    def _(t):
        z_send(t).start()

    acc[...] = jnp.zeros_like(acc)

    @pl.loop(1, ndoc)
    def _(t):
        slab = kvbuf.at[pl.ds(lax.rem(d - t + ndoc, ndoc) * n, n)]
        pltpu.make_async_copy(slab, slab, zr.at[t]).wait()

    both = kvbuf[...].astype(jnp.float32)
    keys[...] = both[:, :rows_p].reshape(total, width).astype(jnp.bfloat16)
    values[...] = both[:, rows_p:].reshape(total, width).astype(jnp.bfloat16)

    scale = HD ** (-0.5)

    def step(s, carry):
        p = source(c, s, n)
        pltpu.make_async_copy(qbuf.at[p], qbuf.at[p], qr.at[p]).wait()
        pltpu.make_async_copy(gbuf.at[p], gbuf.at[p], gr.at[p]).wait()
        for h in range(nheads):
            at = slice(h * HD, (h + 1) * HD)
            q, g = qbuf[p, :, at], gbuf[p, :, at]
            k, v = keys[:, at], values[:, at]
            expo = jnp.exp(dot(k, q, NT) * scale)
            if rows_p != rows:
                place = lax.broadcasted_iota(jnp.int32, expo.shape, 0)
                expo = jnp.where(lax.rem(place, rows_p) < rows, expo, 0.0)
            dprob = dot(v, g, NT)
            norm = jnp.sum(expo, axis=0, keepdims=True)
            drift = jnp.sum(expo * dprob, axis=0, keepdims=True) / norm
            prob = expo * (1.0 / norm)
            dscore = prob * (dprob - drift) * scale
            ds_hi, ds_lo = split16(dscore)
            pr_hi, pr_lo = split16(prob)
            gqbuf[p, :, at] = dot(ds_hi, k, TN) + dot(ds_lo, k, TN)
            grad_k = dot(ds_hi, q, NN) + dot(ds_lo, q, NN)
            grad_v = dot(pr_hi, g, NN) + dot(pr_lo, g, NN)
            acc[:, :rows_p, at] += grad_k.reshape(ndoc * n, rows_p, HD)
            acc[:, rows_p:, at] += grad_v.reshape(ndoc * n, rows_p, HD)

        @pl.when(s > 0)
        def _():
            o_send(p).start()

        return carry

    lax.fori_loop(0, n, step, 0)

    @pl.loop(1, ndoc)
    def _(t):
        r_send(t).start()

    gq_own = pltpu.make_async_copy(gqbuf.at[c], gq_out.at[:, cols(c)], orr.at[c])
    gq_own.start()
    fin_src[...] = acc[pl.ds(d * n, n)]

    @pl.loop(1, ndoc)
    def _(t):
        r_send(t).wait_recv()
        fin_src[...] += rsbuf[t]

    @pl.loop(1, n)
    def _(s):
        f_send(partner(c, s, n)).start()

    fin[c] = fin_src[c]

    @pl.loop(1, n)
    def _(s):
        p = source(c, s, n)
        pltpu.make_async_copy(fin.at[p], fin.at[p], fr.at[p]).wait()

    for i in range(n):
        at = slice(i * width, (i + 1) * width)
        gk_out[:, at] = fin[i, :rows]
        gv_out[:, at] = fin[i, rows_p:rows_p + rows]

    @pl.loop(0, n)
    def _(i):
        mine = gq_out.at[:, cols(i)]
        pltpu.make_async_copy(mine, mine, orr.at[i]).wait()

    @pl.loop(1, n)
    def _(s):
        p = partner(c, s, n)
        kv_send(p).wait_send()
        q_send(p).wait_send()
        g_send(p).wait_send()
        o_send(p).wait_send()
        f_send(p).wait_send()

    @pl.loop(1, ndoc)
    def _(t):
        z_send(t).wait_send()
        r_send(t).wait_send()


def shards(queries, out_grad, mem_keys, mem_values):
    n, ndoc = lax.axis_size("ctx"), lax.axis_size("doc")
    qrows, features = queries.shape[1:]
    rows = mem_keys.shape[1]
    rows_p = -(-rows // 8) * 8
    width = features // n
    slabs = ndoc * n
    pad = ((0, rows_p - rows), (0, 0))
    kv = jnp.concatenate([jnp.pad(mem_keys[0], pad), jnp.pad(mem_values[0], pad)], axis=0)
    dma = pltpu.SemaphoreType.DMA
    vmem = pl.BlockSpec(memory_space=pltpu.VMEM)
    hbm = pl.BlockSpec(memory_space=pl.ANY)
    pairs = slabs * rows_p * n * qrows * width
    gq, gk, gv = pl.pallas_call(
        functools.partial(kernel, n, ndoc, rows, rows_p),
        out_shape=(
            jax.ShapeDtypeStruct((qrows, features), jnp.float32),
            jax.ShapeDtypeStruct((rows, features), jnp.float32),
            jax.ShapeDtypeStruct((rows, features), jnp.float32),
        ),
        in_specs=[hbm, hbm, hbm],
        out_specs=(hbm, vmem, vmem),
        scratch_shapes=[
            pltpu.VMEM((n, qrows, width), jnp.bfloat16),
            pltpu.VMEM((n, qrows, width), jnp.bfloat16),
            pltpu.VMEM((slabs, 2 * rows_p, width), jnp.bfloat16),
            pltpu.VMEM((slabs * rows_p, width), jnp.bfloat16),
            pltpu.VMEM((slabs * rows_p, width), jnp.bfloat16),
            pltpu.VMEM((n, qrows, width), jnp.float32),
            pltpu.VMEM((slabs, 2 * rows_p, width), jnp.float32),
            pltpu.VMEM((ndoc, n, 2 * rows_p, width), jnp.float32),
            pltpu.VMEM((n, 2 * rows_p, width), jnp.float32),
            pltpu.VMEM((n, 2 * rows_p, width), jnp.float32),
            dma((n,)), dma((n,)), dma((n,)), dma((n,)), dma((n,)), dma((n,)),
            dma((ndoc,)), dma((ndoc,)), dma((n,)), dma((n,)),
            dma((ndoc,)), dma((ndoc,)), dma((n,)), dma((n,)),
        ],
        compiler_params=pltpu.CompilerParams(
            collective_id=0, has_side_effects=True, vmem_limit_bytes=48 * 1024 * 1024),
        cost_estimate=pl.CostEstimate(
            flops=16 * pairs, bytes_accessed=8 * qrows * features, transcendentals=pairs // HD),
    )(queries[0], out_grad[0], kv)
    return gq[None], gk[None], gv[None]


def solution(mesh):
    placed = P("doc", "ctx", None)
    return jax.shard_map(
        shards,
        mesh=mesh,
        in_specs=(placed,) * 4,
        out_specs=(placed,) * 3,
        check_vma=False,
    )
```

```python
import functools

import jax
import jax.numpy as jnp
from jax import lax
from jax.experimental import pallas as pl
from jax.experimental.pallas import tpu as pltpu
from jax.sharding import PartitionSpec as P

HD = 128
MESH = pl.DeviceIdType.MESH
NT = (((1,), (1,)), ((), ()))
NN = (((1,), (0,)), ((), ()))
TN = (((0,), (0,)), ((), ()))


def dot(a, b, dims):
    return lax.dot_general(a, b, dims, preferred_element_type=jnp.float32)


def partner(me, step, n):
    if n & (n - 1):
        return lax.rem(me + step, n)
    out, bit = 0, 1
    while bit < n:
        out = out + ((me // bit + step // bit) % 2) * bit
        bit *= 2
    return out


def source(me, step, n):
    if n & (n - 1):
        return lax.rem(me - step + n, n)
    return partner(me, step, n)


TOP = 2.0 ** 15.5


def peak_of(x, axis):
    return jnp.maximum(jnp.max(jnp.abs(x), axis=axis, keepdims=True), 1e-30)


def encode(x, peak):
    y = x * (TOP / peak)
    y = y * y
    y = y * y
    y = y * y
    return jnp.where(x < 0, -y, y).astype(jnp.bfloat16)


def decode(y, peak):
    y = y.astype(jnp.float32)
    fourth = lax.rsqrt(lax.rsqrt(jnp.maximum(jnp.abs(y), 1e-37)))
    x = fourth * lax.rsqrt(fourth) * (peak * (1.0 / TOP))
    return jnp.where(y < 0, -x, x)


def split16(x):
    high = x.astype(jnp.bfloat16)
    return high, (x - high.astype(jnp.float32)).astype(jnp.bfloat16)


def kernel(
    n, ndoc, rows, rows_p,
    q_ref, g_ref, kv_ref,
    gq_out, gqp_out, gkv_out,
    qbuf, gbuf, kvbuf, keys, values, gqbuf, gqp, acc, part, partp, rsbuf, rspbuf, fin_src, fin,
    kvs, kvr, qs, qr, gs, gr, zs, zr, os, orr, ps, pr, rs, rr, ts, tr, fs, fr,
):
    c = lax.axis_index("ctx")
    d = lax.axis_index("doc")
    width = qbuf.shape[2]
    nheads = width // HD
    total = ndoc * n * rows_p

    def cols(i):
        return pl.ds(pl.multiple_of(i * width, width), width)

    barrier = pltpu.get_barrier_semaphore()

    @pl.loop(1, n)
    def _(s):
        pl.semaphore_signal(barrier, inc=1, device_id=(d, lax.rem(c + s, n)), device_id_type=MESH)

    @pl.loop(1, ndoc)
    def _(t):
        pl.semaphore_signal(barrier, inc=1, device_id=(lax.rem(d + t, ndoc), c), device_id_type=MESH)

    pl.semaphore_wait(barrier, n - 1 + ndoc - 1)

    def kv_send(p):
        return pltpu.make_async_remote_copy(
            src_ref=kv_ref.at[:, cols(p)], dst_ref=kvbuf.at[d * n + c],
            send_sem=kvs.at[p], recv_sem=kvr.at[c], device_id=(d, p), device_id_type=MESH)

    def q_send(p):
        return pltpu.make_async_remote_copy(
            src_ref=q_ref.at[:, cols(p)], dst_ref=qbuf.at[c],
            send_sem=qs.at[p], recv_sem=qr.at[c], device_id=(d, p), device_id_type=MESH)

    def g_send(p):
        return pltpu.make_async_remote_copy(
            src_ref=g_ref.at[:, cols(p)], dst_ref=gbuf.at[c],
            send_sem=gs.at[p], recv_sem=gr.at[c], device_id=(d, p), device_id_type=MESH)

    def z_send(t):
        return pltpu.make_async_remote_copy(
            src_ref=kvbuf.at[pl.ds(d * n, n)], dst_ref=kvbuf.at[pl.ds(d * n, n)],
            send_sem=zs.at[t], recv_sem=zr.at[t],
            device_id=(lax.rem(d + t, ndoc), c), device_id_type=MESH)

    def o_send(p):
        return pltpu.make_async_remote_copy(
            src_ref=gqbuf.at[p], dst_ref=gq_out.at[:, cols(c)],
            send_sem=os.at[p], recv_sem=orr.at[c], device_id=(d, p), device_id_type=MESH)

    def p_send(p):
        return pltpu.make_async_remote_copy(
            src_ref=gqp.at[p], dst_ref=gqp_out.at[:, cols(c)],
            send_sem=ps.at[p], recv_sem=pr.at[c], device_id=(d, p), device_id_type=MESH)

    def r_send(t):
        to = lax.rem(d + t, ndoc)
        return pltpu.make_async_remote_copy(
            src_ref=part.at[pl.ds(to * n, n)], dst_ref=rsbuf.at[t],
            send_sem=rs.at[t], recv_sem=rr.at[t], device_id=(to, c), device_id_type=MESH)

    def t_send(t):
        return pltpu.make_async_remote_copy(
            src_ref=partp, dst_ref=rspbuf.at[t],
            send_sem=ts.at[t], recv_sem=tr.at[t],
            device_id=(lax.rem(d + t, ndoc), c), device_id_type=MESH)

    def f_send(p):
        return pltpu.make_async_remote_copy(
            src_ref=fin_src.at[p], dst_ref=fin.at[c],
            send_sem=fs.at[p], recv_sem=fr.at[c], device_id=(d, p), device_id_type=MESH)

    kv_own = pltpu.make_async_copy(kv_ref.at[:, cols(c)], kvbuf.at[d * n + c], kvr.at[c])
    q_own = pltpu.make_async_copy(q_ref.at[:, cols(c)], qbuf.at[c], qr.at[c])
    g_own = pltpu.make_async_copy(g_ref.at[:, cols(c)], gbuf.at[c], gr.at[c])
    kv_own.start()

    @pl.loop(1, n)
    def _(s):
        kv_send(partner(c, s, n)).start()

    q_own.start()
    g_own.start()

    @pl.loop(1, n)
    def _(s):
        p = partner(c, s, n)
        q_send(p).start()
        g_send(p).start()

    @pl.loop(0, n)
    def _(i):
        slab = kvbuf.at[d * n + i]
        pltpu.make_async_copy(slab, slab, kvr.at[i]).wait()

    @pl.loop(1, ndoc)
    def _(t):
        z_send(t).start()

    acc[...] = jnp.zeros_like(acc)

    @pl.loop(1, ndoc)
    def _(t):
        slab = kvbuf.at[pl.ds(lax.rem(d - t + ndoc, ndoc) * n, n)]
        pltpu.make_async_copy(slab, slab, zr.at[t]).wait()

    both = kvbuf[...].astype(jnp.float32)
    keys[...] = both[:, :rows_p].reshape(total, width).astype(jnp.bfloat16)
    values[...] = both[:, rows_p:].reshape(total, width).astype(jnp.bfloat16)

    scale = HD ** (-0.5)

    def step(s, carry):
        p = source(c, s, n)
        pltpu.make_async_copy(qbuf.at[p], qbuf.at[p], qr.at[p]).wait()
        pltpu.make_async_copy(gbuf.at[p], gbuf.at[p], gr.at[p]).wait()
        for h in range(nheads):
            at = slice(h * HD, (h + 1) * HD)
            q, g = qbuf[p, :, at], gbuf[p, :, at]
            k, v = keys[:, at], values[:, at]
            expo = jnp.exp(dot(k, q, NT) * scale)
            if rows_p != rows:
                place = lax.broadcasted_iota(jnp.int32, expo.shape, 0)
                expo = jnp.where(lax.rem(place, rows_p) < rows, expo, 0.0)
            dprob = dot(v, g, NT)
            norm = jnp.sum(expo, axis=0, keepdims=True)
            drift = jnp.sum(expo * dprob, axis=0, keepdims=True) / norm
            prob = expo * (1.0 / norm)
            dscore = prob * (dprob - drift) * scale
            ds_hi, ds_lo = split16(dscore)
            pr_hi, pr_lo = split16(prob)
            grad_q = dot(ds_hi, k, TN) + dot(ds_lo, k, TN)
            peak = peak_of(grad_q, 0)
            gqp[p, :, at] = jnp.broadcast_to(peak, (8, HD))
            gqbuf[p, :, at] = encode(grad_q, peak)
            grad_k = dot(ds_hi, q, NN) + dot(ds_lo, q, NN)
            grad_v = dot(pr_hi, g, NN) + dot(pr_lo, g, NN)
            acc[:, :rows_p, at] += grad_k.reshape(ndoc * n, rows_p, HD)
            acc[:, rows_p:, at] += grad_v.reshape(ndoc * n, rows_p, HD)

        @pl.when(s > 0)
        def _():
            o_send(p).start()
            p_send(p).start()

        return carry

    lax.fori_loop(0, n, step, 0)

    peak_k = peak_of(acc[:, :rows_p].reshape(total, width), 0)
    peak_v = peak_of(acc[:, rows_p:].reshape(total, width), 0)
    partp[...] = jnp.where(lax.broadcasted_iota(jnp.int32, (8, width), 0) < 4, peak_k, peak_v)
    lower = lax.broadcasted_iota(jnp.int32, (2 * rows_p, width), 0) < rows_p
    peaks = jnp.where(lower, peak_k, peak_v)

    @pl.loop(1, ndoc)
    def _(t):
        to = pl.ds(lax.rem(d + t, ndoc) * n, n)
        part[to] = encode(acc[to], peaks[None])
        t_send(t).start()
        r_send(t).start()

    gq_own = pltpu.make_async_copy(gqbuf.at[c], gq_out.at[:, cols(c)], orr.at[c])
    gq_own.start()
    gqp_own = pltpu.make_async_copy(gqp.at[c], gqp_out.at[:, cols(c)], pr.at[c])
    gqp_own.start()
    fin_src[...] = acc[pl.ds(d * n, n)]

    @pl.loop(1, ndoc)
    def _(t):
        t_send(t).wait_recv()
        r_send(t).wait_recv()
        far = jnp.where(lower, rspbuf[t, 0:1], rspbuf[t, 4:5])
        fin_src[...] += decode(rsbuf[t], far[None])

    @pl.loop(1, n)
    def _(s):
        f_send(partner(c, s, n)).start()

    fin[c] = fin_src[c]

    @pl.loop(1, n)
    def _(s):
        p = source(c, s, n)
        pltpu.make_async_copy(fin.at[p], fin.at[p], fr.at[p]).wait()

    for i in range(n):
        at = slice(i * width, (i + 1) * width)
        gkv_out[:, at] = fin[i]

    @pl.loop(0, n)
    def _(i):
        mine = gq_out.at[:, cols(i)]
        pltpu.make_async_copy(mine, mine, orr.at[i]).wait()
        peaks_in = gqp_out.at[:, cols(i)]
        pltpu.make_async_copy(peaks_in, peaks_in, pr.at[i]).wait()

    @pl.loop(1, n)
    def _(s):
        p = partner(c, s, n)
        kv_send(p).wait_send()
        q_send(p).wait_send()
        g_send(p).wait_send()
        o_send(p).wait_send()
        p_send(p).wait_send()
        f_send(p).wait_send()

    @pl.loop(1, ndoc)
    def _(t):
        z_send(t).wait_send()
        r_send(t).wait_send()
        t_send(t).wait_send()


def shards(queries, out_grad, mem_keys, mem_values):
    n, ndoc = lax.axis_size("ctx"), lax.axis_size("doc")
    qrows, features = queries.shape[1:]
    rows = mem_keys.shape[1]
    rows_p = -(-rows // 8) * 8
    width = features // n
    slabs = ndoc * n
    pad = ((0, rows_p - rows), (0, 0))
    kv = jnp.concatenate([jnp.pad(mem_keys[0], pad), jnp.pad(mem_values[0], pad)], axis=0)
    dma = pltpu.SemaphoreType.DMA
    vmem = pl.BlockSpec(memory_space=pltpu.VMEM)
    hbm = pl.BlockSpec(memory_space=pl.ANY)
    pairs = slabs * rows_p * n * qrows * width
    gq, gqp, gkv = pl.pallas_call(
        functools.partial(kernel, n, ndoc, rows, rows_p),
        out_shape=(
            jax.ShapeDtypeStruct((qrows, features), jnp.bfloat16),
            jax.ShapeDtypeStruct((8, features), jnp.float32),
            jax.ShapeDtypeStruct((2 * rows_p, features), jnp.float32),
        ),
        in_specs=[hbm, hbm, hbm],
        out_specs=(vmem, vmem, vmem),
        scratch_shapes=[
            pltpu.VMEM((n, qrows, width), jnp.bfloat16),
            pltpu.VMEM((n, qrows, width), jnp.bfloat16),
            pltpu.VMEM((slabs, 2 * rows_p, width), jnp.bfloat16),
            pltpu.VMEM((slabs * rows_p, width), jnp.bfloat16),
            pltpu.VMEM((slabs * rows_p, width), jnp.bfloat16),
            pltpu.VMEM((n, qrows, width), jnp.bfloat16),
            pltpu.VMEM((n, 8, width), jnp.float32),
            pltpu.VMEM((slabs, 2 * rows_p, width), jnp.float32),
            pltpu.VMEM((slabs, 2 * rows_p, width), jnp.bfloat16),
            pltpu.VMEM((8, width), jnp.float32),
            pltpu.VMEM((ndoc, n, 2 * rows_p, width), jnp.bfloat16),
            pltpu.VMEM((ndoc, 8, width), jnp.float32),
            pltpu.VMEM((n, 2 * rows_p, width), jnp.float32),
            pltpu.VMEM((n, 2 * rows_p, width), jnp.float32),
            dma((n,)), dma((n,)), dma((n,)), dma((n,)), dma((n,)), dma((n,)),
            dma((ndoc,)), dma((ndoc,)), dma((n,)), dma((n,)), dma((n,)), dma((n,)),
            dma((ndoc,)), dma((ndoc,)), dma((ndoc,)), dma((ndoc,)), dma((n,)), dma((n,)),
        ],
        compiler_params=pltpu.CompilerParams(
            collective_id=0, has_side_effects=True, vmem_limit_bytes=58 * 1024 * 1024),
        cost_estimate=pl.CostEstimate(
            flops=16 * pairs, bytes_accessed=8 * qrows * features, transcendentals=pairs // HD),
    )(queries[0], out_grad[0], kv)
    gq = decode(gq, gqp[0:1])
    return gq[None], gkv[None, :rows], gkv[None, rows_p:rows_p + rows]


def solution(mesh):
    placed = P("doc", "ctx", None)
    return jax.shard_map(
        shards,
        mesh=mesh,
        in_specs=(placed,) * 4,
        out_specs=(placed,) * 3,
        check_vma=False,
    )
```

```python
import functools

import jax
import jax.numpy as jnp
from jax import lax
from jax.experimental import pallas as pl
from jax.experimental.pallas import tpu as pltpu
from jax.sharding import PartitionSpec as P

HD = 128
MESH = pl.DeviceIdType.MESH
NT = (((1,), (1,)), ((), ()))
NN = (((1,), (0,)), ((), ()))
TN = (((0,), (0,)), ((), ()))


def dot(a, b, dims):
    return lax.dot_general(a, b, dims, preferred_element_type=jnp.float32)


def partner(me, step, n):
    if n & (n - 1):
        return lax.rem(me + step, n)
    out, bit = 0, 1
    while bit < n:
        out = out + ((me // bit + step // bit) % 2) * bit
        bit *= 2
    return out


def source(me, step, n):
    if n & (n - 1):
        return lax.rem(me - step + n, n)
    return partner(me, step, n)


TOP = 2.0 ** 15.5


def peak_of(x, axis):
    return jnp.maximum(jnp.max(jnp.abs(x), axis=axis, keepdims=True), 1e-30)


def encode(x, peak):
    y = x * (TOP / peak)
    y = y * y
    y = y * y
    y = y * y
    return jnp.where(x < 0, -y, y).astype(jnp.bfloat16)


def decode(y, peak):
    y = y.astype(jnp.float32)
    fourth = lax.rsqrt(lax.rsqrt(jnp.maximum(jnp.abs(y), 1e-37)))
    x = fourth * lax.rsqrt(fourth) * (peak * (1.0 / TOP))
    return jnp.where(y < 0, -x, x)


def split16(x):
    high = x.astype(jnp.bfloat16)
    return high, (x - high.astype(jnp.float32)).astype(jnp.bfloat16)


def kernel(
    n, ndoc, rows, rows_p,
    q_ref, g_ref, kv_ref,
    gq_out, gqp_out, gkv_out,
    qbuf, gbuf, kvbuf, keys, values, gqbuf, gqp, acc, part, partp, rsbuf, rspbuf, fin_src, fin_enc, finp, fin, fin_peaks,
    kvs, kvr, qs, qr, gs, gr, zs, zr, os, orr, ps, pr, rs, rr, ts, tr, fs, fr, us, ur,
):
    c = lax.axis_index("ctx")
    d = lax.axis_index("doc")
    width = qbuf.shape[2]
    nheads = width // HD
    total = ndoc * n * rows_p

    def cols(i):
        return pl.ds(pl.multiple_of(i * width, width), width)

    barrier = pltpu.get_barrier_semaphore()

    @pl.loop(1, n)
    def _(s):
        pl.semaphore_signal(barrier, inc=1, device_id=(d, lax.rem(c + s, n)), device_id_type=MESH)

    @pl.loop(1, ndoc)
    def _(t):
        pl.semaphore_signal(barrier, inc=1, device_id=(lax.rem(d + t, ndoc), c), device_id_type=MESH)

    pl.semaphore_wait(barrier, n - 1 + ndoc - 1)

    def kv_send(p):
        return pltpu.make_async_remote_copy(
            src_ref=kv_ref.at[:, cols(p)], dst_ref=kvbuf.at[d * n + c],
            send_sem=kvs.at[p], recv_sem=kvr.at[c], device_id=(d, p), device_id_type=MESH)

    def q_send(p):
        return pltpu.make_async_remote_copy(
            src_ref=q_ref.at[:, cols(p)], dst_ref=qbuf.at[c],
            send_sem=qs.at[p], recv_sem=qr.at[c], device_id=(d, p), device_id_type=MESH)

    def g_send(p):
        return pltpu.make_async_remote_copy(
            src_ref=g_ref.at[:, cols(p)], dst_ref=gbuf.at[c],
            send_sem=gs.at[p], recv_sem=gr.at[c], device_id=(d, p), device_id_type=MESH)

    def z_send(t):
        return pltpu.make_async_remote_copy(
            src_ref=kvbuf.at[pl.ds(d * n, n)], dst_ref=kvbuf.at[pl.ds(d * n, n)],
            send_sem=zs.at[t], recv_sem=zr.at[t],
            device_id=(lax.rem(d + t, ndoc), c), device_id_type=MESH)

    def o_send(p):
        return pltpu.make_async_remote_copy(
            src_ref=gqbuf.at[p], dst_ref=gq_out.at[:, cols(c)],
            send_sem=os.at[p], recv_sem=orr.at[c], device_id=(d, p), device_id_type=MESH)

    def p_send(p):
        return pltpu.make_async_remote_copy(
            src_ref=gqp.at[p], dst_ref=gqp_out.at[c],
            send_sem=ps.at[p], recv_sem=pr.at[c], device_id=(d, p), device_id_type=MESH)

    def r_send(t):
        to = lax.rem(d + t, ndoc)
        return pltpu.make_async_remote_copy(
            src_ref=part.at[pl.ds(to * n, n)], dst_ref=rsbuf.at[t],
            send_sem=rs.at[t], recv_sem=rr.at[t], device_id=(to, c), device_id_type=MESH)

    def t_send(t):
        return pltpu.make_async_remote_copy(
            src_ref=partp, dst_ref=rspbuf.at[t],
            send_sem=ts.at[t], recv_sem=tr.at[t],
            device_id=(lax.rem(d + t, ndoc), c), device_id_type=MESH)

    def f_send(p):
        return pltpu.make_async_remote_copy(
            src_ref=fin_enc.at[p], dst_ref=fin.at[c],
            send_sem=fs.at[p], recv_sem=fr.at[c], device_id=(d, p), device_id_type=MESH)

    def u_send(p):
        return pltpu.make_async_remote_copy(
            src_ref=finp, dst_ref=fin_peaks.at[c],
            send_sem=us.at[p], recv_sem=ur.at[c], device_id=(d, p), device_id_type=MESH)

    lower = lax.broadcasted_iota(jnp.int32, (2 * rows_p, HD), 0) < rows_p

    def note_peaks(tile, x):
        for first, half in ((0, x[:, :rows_p]), (nheads, x[:, rows_p:])):
            peak = peak_of(half.reshape(-1, width), 0)
            for h in range(nheads):
                tile[first + h:first + h + 1] = peak[:, h * HD:(h + 1) * HD]

    def spread(tile):
        return jnp.concatenate(
            [jnp.where(lower, tile[h:h + 1], tile[nheads + h:nheads + h + 1]) for h in range(nheads)], axis=1)

    kv_own = pltpu.make_async_copy(kv_ref.at[:, cols(c)], kvbuf.at[d * n + c], kvr.at[c])
    q_own = pltpu.make_async_copy(q_ref.at[:, cols(c)], qbuf.at[c], qr.at[c])
    g_own = pltpu.make_async_copy(g_ref.at[:, cols(c)], gbuf.at[c], gr.at[c])
    kv_own.start()

    @pl.loop(1, n)
    def _(s):
        kv_send(partner(c, s, n)).start()

    q_own.start()
    g_own.start()

    @pl.loop(1, n)
    def _(s):
        p = partner(c, s, n)
        q_send(p).start()
        g_send(p).start()

    @pl.loop(0, n)
    def _(i):
        slab = kvbuf.at[d * n + i]
        pltpu.make_async_copy(slab, slab, kvr.at[i]).wait()

    @pl.loop(1, ndoc)
    def _(t):
        z_send(t).start()

    acc[...] = jnp.zeros_like(acc)
    gqp[...] = jnp.zeros_like(gqp)
    partp[...] = jnp.zeros_like(partp)
    finp[...] = jnp.zeros_like(finp)

    @pl.loop(1, ndoc)
    def _(t):
        slab = kvbuf.at[pl.ds(lax.rem(d - t + ndoc, ndoc) * n, n)]
        pltpu.make_async_copy(slab, slab, zr.at[t]).wait()

    both = kvbuf[...].astype(jnp.float32)
    keys[...] = both[:, :rows_p].reshape(total, width).astype(jnp.bfloat16)
    values[...] = both[:, rows_p:].reshape(total, width).astype(jnp.bfloat16)

    scale = HD ** (-0.5)

    def step(s, carry):
        p = source(c, s, n)
        pltpu.make_async_copy(qbuf.at[p], qbuf.at[p], qr.at[p]).wait()
        pltpu.make_async_copy(gbuf.at[p], gbuf.at[p], gr.at[p]).wait()
        for h in range(nheads):
            at = slice(h * HD, (h + 1) * HD)
            q, g = qbuf[p, :, at], gbuf[p, :, at]
            k, v = keys[:, at], values[:, at]
            expo = jnp.exp(dot(k, q, NT) * scale)
            if rows_p != rows:
                place = lax.broadcasted_iota(jnp.int32, expo.shape, 0)
                expo = jnp.where(lax.rem(place, rows_p) < rows, expo, 0.0)
            dprob = dot(v, g, NT)
            norm = jnp.sum(expo, axis=0, keepdims=True)
            drift = jnp.sum(expo * dprob, axis=0, keepdims=True) / norm
            prob = expo * (1.0 / norm)
            dscore = prob * (dprob - drift) * scale
            ds_hi, ds_lo = split16(dscore)
            pr_hi, pr_lo = split16(prob)
            grad_q = dot(ds_hi, k, TN) + dot(ds_lo, k, TN)
            peak = peak_of(grad_q, 0)
            gqp[p, h:h + 1] = peak
            gqbuf[p, :, at] = encode(grad_q, peak)
            grad_k = dot(ds_hi, q, NN) + dot(ds_lo, q, NN)
            grad_v = dot(pr_hi, g, NN) + dot(pr_lo, g, NN)
            acc[:, :rows_p, at] += grad_k.reshape(ndoc * n, rows_p, HD)
            acc[:, rows_p:, at] += grad_v.reshape(ndoc * n, rows_p, HD)

        @pl.when(s > 0)
        def _():
            o_send(p).start()
            p_send(p).start()

        return carry

    lax.fori_loop(0, n, step, 0)

    note_peaks(partp, acc[...])
    peaks = spread(partp[...])

    @pl.loop(1, ndoc)
    def _(t):
        to = pl.ds(lax.rem(d + t, ndoc) * n, n)
        part[to] = encode(acc[to], peaks[None])
        t_send(t).start()
        r_send(t).start()

    gq_own = pltpu.make_async_copy(gqbuf.at[c], gq_out.at[:, cols(c)], orr.at[c])
    gq_own.start()
    gqp_own = pltpu.make_async_copy(gqp.at[c], gqp_out.at[c], pr.at[c])
    gqp_own.start()
    fin_src[...] = acc[pl.ds(d * n, n)]

    @pl.loop(1, ndoc)
    def _(t):
        t_send(t).wait_recv()
        r_send(t).wait_recv()
        fin_src[...] += decode(rsbuf[t], spread(rspbuf[t])[None])

    note_peaks(finp, fin_src[...])
    fin_enc[...] = encode(fin_src[...], spread(finp[...])[None])

    @pl.loop(1, n)
    def _(s):
        p = partner(c, s, n)
        u_send(p).start()
        f_send(p).start()

    fin[c] = fin_enc[c]
    fin_peaks[c] = finp[...]

    @pl.loop(1, n)
    def _(s):
        p = source(c, s, n)
        pltpu.make_async_copy(fin.at[p], fin.at[p], fr.at[p]).wait()
        pltpu.make_async_copy(fin_peaks.at[p], fin_peaks.at[p], ur.at[p]).wait()

    for i in range(n):
        at = slice(i * width, (i + 1) * width)
        gkv_out[:, at] = decode(fin[i], spread(fin_peaks[i]))

    @pl.loop(0, n)
    def _(i):
        mine = gq_out.at[:, cols(i)]
        pltpu.make_async_copy(mine, mine, orr.at[i]).wait()
        peaks_in = gqp_out.at[i]
        pltpu.make_async_copy(peaks_in, peaks_in, pr.at[i]).wait()

    @pl.loop(1, n)
    def _(s):
        p = partner(c, s, n)
        kv_send(p).wait_send()
        q_send(p).wait_send()
        g_send(p).wait_send()
        o_send(p).wait_send()
        p_send(p).wait_send()
        f_send(p).wait_send()
        u_send(p).wait_send()

    @pl.loop(1, ndoc)
    def _(t):
        z_send(t).wait_send()
        r_send(t).wait_send()
        t_send(t).wait_send()


def up8(x):
    return -(-x // 8) * 8


def shards(queries, out_grad, mem_keys, mem_values):
    n, ndoc = lax.axis_size("ctx"), lax.axis_size("doc")
    qrows, features = queries.shape[1:]
    rows = mem_keys.shape[1]
    rows_p = up8(rows)
    width = features // n
    nheads = width // HD
    slabs = ndoc * n
    pad = ((0, rows_p - rows), (0, 0))
    kv = jnp.concatenate([jnp.pad(mem_keys[0], pad), jnp.pad(mem_values[0], pad)], axis=0)
    dma = pltpu.SemaphoreType.DMA
    vmem = pl.BlockSpec(memory_space=pltpu.VMEM)
    hbm = pl.BlockSpec(memory_space=pl.ANY)
    pairs = slabs * rows_p * n * qrows * width
    gq, gqp, gkv = pl.pallas_call(
        functools.partial(kernel, n, ndoc, rows, rows_p),
        out_shape=(
            jax.ShapeDtypeStruct((qrows, features), jnp.bfloat16),
            jax.ShapeDtypeStruct((n, up8(nheads), HD), jnp.float32),
            jax.ShapeDtypeStruct((2 * rows_p, features), jnp.float32),
        ),
        in_specs=[hbm, hbm, hbm],
        out_specs=(vmem, vmem, vmem),
        scratch_shapes=[
            pltpu.VMEM((n, qrows, width), jnp.bfloat16),
            pltpu.VMEM((n, qrows, width), jnp.bfloat16),
            pltpu.VMEM((slabs, 2 * rows_p, width), jnp.bfloat16),
            pltpu.VMEM((slabs * rows_p, width), jnp.bfloat16),
            pltpu.VMEM((slabs * rows_p, width), jnp.bfloat16),
            pltpu.VMEM((n, qrows, width), jnp.bfloat16),
            pltpu.VMEM((n, up8(nheads), HD), jnp.float32),
            pltpu.VMEM((slabs, 2 * rows_p, width), jnp.float32),
            pltpu.VMEM((slabs, 2 * rows_p, width), jnp.bfloat16),
            pltpu.VMEM((up8(2 * nheads), HD), jnp.float32),
            pltpu.VMEM((ndoc, n, 2 * rows_p, width), jnp.bfloat16),
            pltpu.VMEM((ndoc, up8(2 * nheads), HD), jnp.float32),
            pltpu.VMEM((n, 2 * rows_p, width), jnp.float32),
            pltpu.VMEM((n, 2 * rows_p, width), jnp.bfloat16),
            pltpu.VMEM((up8(2 * nheads), HD), jnp.float32),
            pltpu.VMEM((n, 2 * rows_p, width), jnp.bfloat16),
            pltpu.VMEM((n, up8(2 * nheads), HD), jnp.float32),
            dma((n,)), dma((n,)), dma((n,)), dma((n,)), dma((n,)), dma((n,)),
            dma((ndoc,)), dma((ndoc,)), dma((n,)), dma((n,)), dma((n,)), dma((n,)),
            dma((ndoc,)), dma((ndoc,)), dma((ndoc,)), dma((ndoc,)), dma((n,)), dma((n,)),
            dma((n,)), dma((n,)),
        ],
        compiler_params=pltpu.CompilerParams(
            collective_id=0, has_side_effects=True, vmem_limit_bytes=58 * 1024 * 1024),
        cost_estimate=pl.CostEstimate(
            flops=16 * pairs, bytes_accessed=8 * qrows * features, transcendentals=pairs // HD),
    )(queries[0], out_grad[0], kv)
    gq = decode(gq, gqp[:, :nheads].reshape(1, features))
    return gq[None], gkv[None, :rows], gkv[None, rows_p:rows_p + rows]


def solution(mesh):
    placed = P("doc", "ctx", None)
    return jax.shard_map(
        shards,
        mesh=mesh,
        in_specs=(placed,) * 4,
        out_specs=(placed,) * 3,
        check_vma=False,
    )
```

```python
import functools

import jax
import jax.numpy as jnp
from jax import lax
from jax.experimental import pallas as pl
from jax.experimental.pallas import tpu as pltpu
from jax.sharding import PartitionSpec as P

HD = 128
MESH = pl.DeviceIdType.MESH
NT = (((1,), (1,)), ((), ()))
NN = (((1,), (0,)), ((), ()))
TN = (((0,), (0,)), ((), ()))


def dot(a, b, dims):
    return lax.dot_general(a, b, dims, preferred_element_type=jnp.float32)


def partner(me, step, n):
    if n & (n - 1):
        return lax.rem(me + step, n)
    out, bit = 0, 1
    while bit < n:
        out = out + ((me // bit + step // bit) % 2) * bit
        bit *= 2
    return out


def source(me, step, n):
    if n & (n - 1):
        return lax.rem(me - step + n, n)
    return partner(me, step, n)


TOP = 2.0 ** 15.5


def peak_of(x, axis):
    return jnp.maximum(jnp.max(jnp.abs(x), axis=axis, keepdims=True), 1e-30)


def encode(x, peak):
    y = x * (TOP / peak)
    y = y * y
    y = y * y
    y = y * y
    return jnp.where(x < 0, -y, y).astype(jnp.bfloat16)


def decode(y, peak):
    y = y.astype(jnp.float32)
    fourth = lax.rsqrt(lax.rsqrt(jnp.maximum(jnp.abs(y), 1e-37)))
    x = fourth * lax.rsqrt(fourth) * (peak * (1.0 / TOP))
    return jnp.where(y < 0, -x, x)


def split16(x):
    high = x.astype(jnp.bfloat16)
    return high, (x - high.astype(jnp.float32)).astype(jnp.bfloat16)


def kernel(
    n, ndoc, rows, rows_p,
    q_ref, g_ref, kv_ref,
    gq_out, gqp_out, gkv_out,
    qbuf, gbuf, kvbuf, keys, values, gqbuf, gqp, acc, part, partp, rsbuf, rspbuf, fin_src, fin_enc, finp, fin, fin_peaks,
    kvs, kvr, qs, qr, gs, gr, zs, zr, os, orr, ps, pr, rs, rr, ts, tr, fs, fr, us, ur,
):
    c = lax.axis_index("ctx")
    d = lax.axis_index("doc")
    halves, part_w = qbuf.shape[0], qbuf.shape[3]
    width = halves * part_w
    nheads = width // HD
    few = part_w // HD
    total = ndoc * n * rows_p

    def cols(i):
        return pl.ds(pl.multiple_of(i * width, width), width)

    def part_cols(i, a):
        return pl.ds(pl.multiple_of(i * width + a * part_w, part_w), part_w)

    barrier = pltpu.get_barrier_semaphore()

    @pl.loop(1, n)
    def _(s):
        pl.semaphore_signal(barrier, inc=1, device_id=(d, lax.rem(c + s, n)), device_id_type=MESH)

    @pl.loop(1, ndoc)
    def _(t):
        pl.semaphore_signal(barrier, inc=1, device_id=(lax.rem(d + t, ndoc), c), device_id_type=MESH)

    pl.semaphore_wait(barrier, n - 1 + ndoc - 1)

    def kv_send(p):
        return pltpu.make_async_remote_copy(
            src_ref=kv_ref.at[:, cols(p)], dst_ref=kvbuf.at[d * n + c],
            send_sem=kvs.at[p], recv_sem=kvr.at[c], device_id=(d, p), device_id_type=MESH)

    def q_send(p, a):
        return pltpu.make_async_remote_copy(
            src_ref=q_ref.at[:, part_cols(p, a)], dst_ref=qbuf.at[a, c],
            send_sem=qs.at[a * n + p], recv_sem=qr.at[a * n + c], device_id=(d, p), device_id_type=MESH)

    def g_send(p, a):
        return pltpu.make_async_remote_copy(
            src_ref=g_ref.at[:, part_cols(p, a)], dst_ref=gbuf.at[a, c],
            send_sem=gs.at[a * n + p], recv_sem=gr.at[a * n + c], device_id=(d, p), device_id_type=MESH)

    def z_send(t):
        return pltpu.make_async_remote_copy(
            src_ref=kvbuf.at[pl.ds(d * n, n)], dst_ref=kvbuf.at[pl.ds(d * n, n)],
            send_sem=zs.at[t], recv_sem=zr.at[t],
            device_id=(lax.rem(d + t, ndoc), c), device_id_type=MESH)

    def o_send(p, a):
        return pltpu.make_async_remote_copy(
            src_ref=gqbuf.at[a, p], dst_ref=gq_out.at[:, part_cols(c, a)],
            send_sem=os.at[a * n + p], recv_sem=orr.at[a * n + c], device_id=(d, p), device_id_type=MESH)

    def p_send(p):
        return pltpu.make_async_remote_copy(
            src_ref=gqp.at[p], dst_ref=gqp_out.at[c],
            send_sem=ps.at[p], recv_sem=pr.at[c], device_id=(d, p), device_id_type=MESH)

    def r_send(t, a):
        to = lax.rem(d + t, ndoc)
        return pltpu.make_async_remote_copy(
            src_ref=part.at[a, pl.ds(to * n, n)], dst_ref=rsbuf.at[a, t],
            send_sem=rs.at[a * ndoc + t], recv_sem=rr.at[a * ndoc + t], device_id=(to, c), device_id_type=MESH)

    def t_send(t, a):
        return pltpu.make_async_remote_copy(
            src_ref=partp.at[a], dst_ref=rspbuf.at[a, t],
            send_sem=ts.at[a * ndoc + t], recv_sem=tr.at[a * ndoc + t],
            device_id=(lax.rem(d + t, ndoc), c), device_id_type=MESH)

    def f_send(p):
        return pltpu.make_async_remote_copy(
            src_ref=fin_enc.at[p], dst_ref=fin.at[c],
            send_sem=fs.at[p], recv_sem=fr.at[c], device_id=(d, p), device_id_type=MESH)

    def u_send(p):
        return pltpu.make_async_remote_copy(
            src_ref=finp, dst_ref=fin_peaks.at[c],
            send_sem=us.at[p], recv_sem=ur.at[c], device_id=(d, p), device_id_type=MESH)

    lower = lax.broadcasted_iota(jnp.int32, (2 * rows_p, HD), 0) < rows_p

    def peaks_of(x):
        count = x.shape[2] // HD
        tops = [peak_of(half.reshape(-1, x.shape[2]), 0) for half in (x[:, :rows_p], x[:, rows_p:])]
        return [top[:, h * HD:(h + 1) * HD] for top in tops for h in range(count)]

    def spread(tile, count):
        return jnp.concatenate(
            [jnp.where(lower, tile[h:h + 1], tile[count + h:count + h + 1]) for h in range(count)], axis=1)

    kv_own = pltpu.make_async_copy(kv_ref.at[:, cols(c)], kvbuf.at[d * n + c], kvr.at[c])
    kv_own.start()

    @pl.loop(1, n)
    def _(s):
        kv_send(partner(c, s, n)).start()

    for a in range(halves):
        pltpu.make_async_copy(q_ref.at[:, part_cols(c, a)], qbuf.at[a, c], qr.at[a * n + c]).start()
    for a in range(halves):
        pltpu.make_async_copy(g_ref.at[:, part_cols(c, a)], gbuf.at[a, c], gr.at[a * n + c]).start()

    for a in range(halves):
        @pl.loop(1, n)
        def _(s, a=a):
            p = partner(c, s, n)
            q_send(p, a).start()
            g_send(p, a).start()

    @pl.loop(0, n)
    def _(i):
        slab = kvbuf.at[d * n + i]
        pltpu.make_async_copy(slab, slab, kvr.at[i]).wait()

    @pl.loop(1, ndoc)
    def _(t):
        z_send(t).start()

    acc[...] = jnp.zeros_like(acc)
    gqp[...] = jnp.zeros_like(gqp)
    partp[...] = jnp.zeros_like(partp)
    finp[...] = jnp.zeros_like(finp)

    @pl.loop(1, ndoc)
    def _(t):
        slab = kvbuf.at[pl.ds(lax.rem(d - t + ndoc, ndoc) * n, n)]
        pltpu.make_async_copy(slab, slab, zr.at[t]).wait()

    both = kvbuf[...].astype(jnp.float32)
    keys[...] = both[:, :rows_p].reshape(total, width).astype(jnp.bfloat16)
    values[...] = both[:, rows_p:].reshape(total, width).astype(jnp.bfloat16)

    scale = HD ** (-0.5)

    def step(a, s, carry):
        p = source(c, s, n)
        pltpu.make_async_copy(qbuf.at[a, p], qbuf.at[a, p], qr.at[a * n + p]).wait()
        pltpu.make_async_copy(gbuf.at[a, p], gbuf.at[a, p], gr.at[a * n + p]).wait()
        for h in range(few):
            near = slice(h * HD, (h + 1) * HD)
            at = slice(a * part_w + h * HD, a * part_w + (h + 1) * HD)
            q, g = qbuf[a, p, :, near], gbuf[a, p, :, near]
            k, v = keys[:, at], values[:, at]
            expo = jnp.exp(dot(k, q, NT) * scale)
            if rows_p != rows:
                place = lax.broadcasted_iota(jnp.int32, expo.shape, 0)
                expo = jnp.where(lax.rem(place, rows_p) < rows, expo, 0.0)
            dprob = dot(v, g, NT)
            norm = jnp.sum(expo, axis=0, keepdims=True)
            drift = jnp.sum(expo * dprob, axis=0, keepdims=True) / norm
            prob = expo * (1.0 / norm)
            dscore = prob * (dprob - drift) * scale
            ds_hi, ds_lo = split16(dscore)
            pr_hi, pr_lo = split16(prob)
            grad_q = dot(ds_hi, k, TN) + dot(ds_lo, k, TN)
            peak = peak_of(grad_q, 0)
            gqp[p, a * few + h:a * few + h + 1] = peak
            gqbuf[a, p, :, near] = encode(grad_q, peak)
            grad_k = dot(ds_hi, q, NN) + dot(ds_lo, q, NN)
            grad_v = dot(pr_hi, g, NN) + dot(pr_lo, g, NN)
            acc[:, :rows_p, at] += grad_k.reshape(ndoc * n, rows_p, HD)
            acc[:, rows_p:, at] += grad_v.reshape(ndoc * n, rows_p, HD)

        @pl.when(s > 0)
        def _():
            o_send(p, a).start()
            if a == halves - 1:
                p_send(p).start()

        return carry

    for a in range(halves):
        lax.fori_loop(0, n, functools.partial(step, a), 0)
        chosen = slice(a * part_w, (a + 1) * part_w)
        tops = peaks_of(acc[:, :, chosen])
        for i, top in enumerate(tops):
            partp[a, i:i + 1] = top
        peaks = spread(partp[a], few)

        @pl.loop(1, ndoc)
        def _(t, a=a, chosen=chosen, peaks=peaks):
            to = pl.ds(lax.rem(d + t, ndoc) * n, n)
            part[a, to] = encode(acc[to, :, chosen], peaks[None])
            t_send(t, a).start()
            r_send(t, a).start()

        pltpu.make_async_copy(gqbuf.at[a, c], gq_out.at[:, part_cols(c, a)], orr.at[a * n + c]).start()

    gqp_own = pltpu.make_async_copy(gqp.at[c], gqp_out.at[c], pr.at[c])
    gqp_own.start()
    fin_src[...] = acc[pl.ds(d * n, n)]

    for a in range(halves):
        chosen = slice(a * part_w, (a + 1) * part_w)

        @pl.loop(1, ndoc)
        def _(t, a=a, chosen=chosen):
            t_send(t, a).wait_recv()
            r_send(t, a).wait_recv()
            fin_src[:, :, chosen] += decode(rsbuf[a, t], spread(rspbuf[a, t], few)[None])

    for i, top in enumerate(peaks_of(fin_src[...])):
        finp[i:i + 1] = top
    fin_enc[...] = encode(fin_src[...], spread(finp[...], nheads)[None])

    @pl.loop(1, n)
    def _(s):
        p = partner(c, s, n)
        u_send(p).start()
        f_send(p).start()

    fin[c] = fin_enc[c]
    fin_peaks[c] = finp[...]

    @pl.loop(1, n)
    def _(s):
        p = source(c, s, n)
        pltpu.make_async_copy(fin.at[p], fin.at[p], fr.at[p]).wait()
        pltpu.make_async_copy(fin_peaks.at[p], fin_peaks.at[p], ur.at[p]).wait()

    for i in range(n):
        at = slice(i * width, (i + 1) * width)
        gkv_out[:, at] = decode(fin[i], spread(fin_peaks[i], nheads))

    @pl.loop(0, n)
    def _(i):
        for a in range(halves):
            mine = gq_out.at[:, part_cols(i, a)]
            pltpu.make_async_copy(mine, mine, orr.at[a * n + i]).wait()
        peaks_in = gqp_out.at[i]
        pltpu.make_async_copy(peaks_in, peaks_in, pr.at[i]).wait()

    @pl.loop(1, n)
    def _(s):
        p = partner(c, s, n)
        kv_send(p).wait_send()
        for a in range(halves):
            q_send(p, a).wait_send()
            g_send(p, a).wait_send()
            o_send(p, a).wait_send()
        p_send(p).wait_send()
        f_send(p).wait_send()
        u_send(p).wait_send()

    @pl.loop(1, ndoc)
    def _(t):
        z_send(t).wait_send()
        for a in range(halves):
            r_send(t, a).wait_send()
            t_send(t, a).wait_send()


def up8(x):
    return -(-x // 8) * 8


def shards(queries, out_grad, mem_keys, mem_values):
    n, ndoc = lax.axis_size("ctx"), lax.axis_size("doc")
    qrows, features = queries.shape[1:]
    rows = mem_keys.shape[1]
    rows_p = up8(rows)
    width = features // n
    nheads = width // HD
    slabs = ndoc * n
    halves = 2 if nheads % 2 == 0 else 1
    few = nheads // halves
    pad = ((0, rows_p - rows), (0, 0))
    kv = jnp.concatenate([jnp.pad(mem_keys[0], pad), jnp.pad(mem_values[0], pad)], axis=0)
    dma = pltpu.SemaphoreType.DMA
    vmem = pl.BlockSpec(memory_space=pltpu.VMEM)
    hbm = pl.BlockSpec(memory_space=pl.ANY)
    pairs = slabs * rows_p * n * qrows * width
    gq, gqp, gkv = pl.pallas_call(
        functools.partial(kernel, n, ndoc, rows, rows_p),
        out_shape=(
            jax.ShapeDtypeStruct((qrows, features), jnp.bfloat16),
            jax.ShapeDtypeStruct((n, up8(nheads), HD), jnp.float32),
            jax.ShapeDtypeStruct((2 * rows_p, features), jnp.float32),
        ),
        in_specs=[hbm, hbm, hbm],
        out_specs=(vmem, vmem, vmem),
        scratch_shapes=[
            pltpu.VMEM((halves, n, qrows, width // halves), jnp.bfloat16),
            pltpu.VMEM((halves, n, qrows, width // halves), jnp.bfloat16),
            pltpu.VMEM((slabs, 2 * rows_p, width), jnp.bfloat16),
            pltpu.VMEM((slabs * rows_p, width), jnp.bfloat16),
            pltpu.VMEM((slabs * rows_p, width), jnp.bfloat16),
            pltpu.VMEM((halves, n, qrows, width // halves), jnp.bfloat16),
            pltpu.VMEM((n, up8(nheads), HD), jnp.float32),
            pltpu.VMEM((slabs, 2 * rows_p, width), jnp.float32),
            pltpu.VMEM((halves, slabs, 2 * rows_p, width // halves), jnp.bfloat16),
            pltpu.VMEM((halves, up8(2 * few), HD), jnp.float32),
            pltpu.VMEM((halves, ndoc, n, 2 * rows_p, width // halves), jnp.bfloat16),
            pltpu.VMEM((halves, ndoc, up8(2 * few), HD), jnp.float32),
            pltpu.VMEM((n, 2 * rows_p, width), jnp.float32),
            pltpu.VMEM((n, 2 * rows_p, width), jnp.bfloat16),
            pltpu.VMEM((up8(2 * nheads), HD), jnp.float32),
            pltpu.VMEM((n, 2 * rows_p, width), jnp.bfloat16),
            pltpu.VMEM((n, up8(2 * nheads), HD), jnp.float32),
            dma((n,)), dma((n,)), *[dma((halves * n,))] * 4,
            dma((ndoc,)), dma((ndoc,)), dma((halves * n,)), dma((halves * n,)), dma((n,)), dma((n,)),
            *[dma((halves * ndoc,))] * 4, dma((n,)), dma((n,)), dma((n,)), dma((n,)),
        ],
        compiler_params=pltpu.CompilerParams(
            collective_id=0, has_side_effects=True, vmem_limit_bytes=58 * 1024 * 1024),
        cost_estimate=pl.CostEstimate(
            flops=16 * pairs, bytes_accessed=8 * qrows * features, transcendentals=pairs // HD),
    )(queries[0], out_grad[0], kv)
    gq = decode(gq, gqp[:, :nheads].reshape(1, features))
    return gq[None], gkv[None, :rows], gkv[None, rows_p:rows_p + rows]


def solution(mesh):
    placed = P("doc", "ctx", None)
    return jax.shard_map(
        shards,
        mesh=mesh,
        in_specs=(placed,) * 4,
        out_specs=(placed,) * 3,
        check_vma=False,
    )
```

```python
import functools

import jax
import jax.numpy as jnp
from jax import lax
from jax.experimental import pallas as pl
from jax.experimental.pallas import tpu as pltpu
from jax.sharding import PartitionSpec as P

HD = 128
MESH = pl.DeviceIdType.MESH
NT = (((1,), (1,)), ((), ()))
NN = (((1,), (0,)), ((), ()))
TN = (((0,), (0,)), ((), ()))


def dot(a, b, dims):
    return lax.dot_general(a, b, dims, preferred_element_type=jnp.float32)


def partner(me, step, n):
    if n & (n - 1):
        return lax.rem(me + step, n)
    out, bit = 0, 1
    while bit < n:
        out = out + ((me // bit + step // bit) % 2) * bit
        bit *= 2
    return out


def source(me, step, n):
    if n & (n - 1):
        return lax.rem(me - step + n, n)
    return partner(me, step, n)


TOP = 2.0 ** 15.5


def peak_of(x, axis):
    return jnp.maximum(jnp.max(jnp.abs(x), axis=axis, keepdims=True), 1e-30)


def encode(x, peak):
    y = x * (TOP / peak)
    y = y * y
    y = y * y
    y = y * y
    return jnp.where(x < 0, -y, y).astype(jnp.bfloat16)


def decode(y, peak):
    y = y.astype(jnp.float32)
    fourth = lax.rsqrt(lax.rsqrt(jnp.maximum(jnp.abs(y), 1e-37)))
    x = fourth * lax.rsqrt(fourth) * (peak * (1.0 / TOP))
    return jnp.where(y < 0, -x, x)


def split16(x):
    high = x.astype(jnp.bfloat16)
    return high, (x - high.astype(jnp.float32)).astype(jnp.bfloat16)


def kernel(
    n, ndoc, rows, rows_p,
    q_ref, g_ref, kv_ref,
    gq_out, gqp_out, gkv_out,
    qbuf, gbuf, kvbuf, keys, values, gqbuf, gqp, acc, part, partp, rsbuf, rspbuf, fin_src, fin_enc, finp, fin, fin_peaks,
    kvs, kvr, qs, qr, gs, gr, zs, zr, os, orr, ps, pr, rs, rr, ts, tr, fs, fr, us, ur,
):
    c = lax.axis_index("ctx")
    d = lax.axis_index("doc")
    halves, part_w = qbuf.shape[0], qbuf.shape[3]
    width = halves * part_w
    nheads = width // HD
    few = part_w // HD
    total = ndoc * n * rows_p

    def cols(i):
        return pl.ds(pl.multiple_of(i * width, width), width)

    def part_cols(i, a):
        return pl.ds(pl.multiple_of(i * width + a * part_w, part_w), part_w)

    barrier = pltpu.get_barrier_semaphore()

    @pl.loop(1, n)
    def _(s):
        pl.semaphore_signal(barrier, inc=1, device_id=(d, lax.rem(c + s, n)), device_id_type=MESH)

    @pl.loop(1, ndoc)
    def _(t):
        pl.semaphore_signal(barrier, inc=1, device_id=(lax.rem(d + t, ndoc), c), device_id_type=MESH)

    pl.semaphore_wait(barrier, n - 1 + ndoc - 1)

    def kv_send(p):
        return pltpu.make_async_remote_copy(
            src_ref=kv_ref.at[:, cols(p)], dst_ref=kvbuf.at[d * n + c],
            send_sem=kvs.at[p], recv_sem=kvr.at[c], device_id=(d, p), device_id_type=MESH)

    def q_send(p, a):
        return pltpu.make_async_remote_copy(
            src_ref=q_ref.at[:, part_cols(p, a)], dst_ref=qbuf.at[a, c],
            send_sem=qs.at[a * n + p], recv_sem=qr.at[a * n + c], device_id=(d, p), device_id_type=MESH)

    def g_send(p, a):
        return pltpu.make_async_remote_copy(
            src_ref=g_ref.at[:, part_cols(p, a)], dst_ref=gbuf.at[a, c],
            send_sem=gs.at[a * n + p], recv_sem=gr.at[a * n + c], device_id=(d, p), device_id_type=MESH)

    def z_send(t):
        return pltpu.make_async_remote_copy(
            src_ref=kvbuf.at[pl.ds(d * n, n)], dst_ref=kvbuf.at[pl.ds(d * n, n)],
            send_sem=zs.at[t], recv_sem=zr.at[t],
            device_id=(lax.rem(d + t, ndoc), c), device_id_type=MESH)

    def o_send(p, a):
        return pltpu.make_async_remote_copy(
            src_ref=gqbuf.at[a, p], dst_ref=gq_out.at[:, part_cols(c, a)],
            send_sem=os.at[a * n + p], recv_sem=orr.at[a * n + c], device_id=(d, p), device_id_type=MESH)

    def p_send(p):
        return pltpu.make_async_remote_copy(
            src_ref=gqp.at[p], dst_ref=gqp_out.at[c],
            send_sem=ps.at[p], recv_sem=pr.at[c], device_id=(d, p), device_id_type=MESH)

    def r_send(t, a):
        to = lax.rem(d + t, ndoc)
        return pltpu.make_async_remote_copy(
            src_ref=part.at[a, pl.ds(to * n, n)], dst_ref=rsbuf.at[a, t],
            send_sem=rs.at[a * ndoc + t], recv_sem=rr.at[a * ndoc + t], device_id=(to, c), device_id_type=MESH)

    def t_send(t, a):
        return pltpu.make_async_remote_copy(
            src_ref=partp.at[a], dst_ref=rspbuf.at[a, t],
            send_sem=ts.at[a * ndoc + t], recv_sem=tr.at[a * ndoc + t],
            device_id=(lax.rem(d + t, ndoc), c), device_id_type=MESH)

    def f_send(p):
        return pltpu.make_async_remote_copy(
            src_ref=fin_enc.at[p], dst_ref=fin.at[c],
            send_sem=fs.at[p], recv_sem=fr.at[c], device_id=(d, p), device_id_type=MESH)

    def u_send(p):
        return pltpu.make_async_remote_copy(
            src_ref=finp, dst_ref=fin_peaks.at[c],
            send_sem=us.at[p], recv_sem=ur.at[c], device_id=(d, p), device_id_type=MESH)

    lower = lax.broadcasted_iota(jnp.int32, (2 * rows_p, HD), 0) < rows_p

    def peaks_of(x):
        count = x.shape[2] // HD
        tops = [peak_of(half.reshape(-1, x.shape[2]), 0) for half in (x[:, :rows_p], x[:, rows_p:])]
        return [top[:, h * HD:(h + 1) * HD] for top in tops for h in range(count)]

    def spread(tile, count):
        return jnp.concatenate(
            [jnp.where(lower, tile[h:h + 1], tile[count + h:count + h + 1]) for h in range(count)], axis=1)

    kv_own = pltpu.make_async_copy(kv_ref.at[:, cols(c)], kvbuf.at[d * n + c], kvr.at[c])
    kv_own.start()

    @pl.loop(1, n)
    def _(s):
        kv_send(partner(c, s, n)).start()

    for a in range(halves):
        pltpu.make_async_copy(q_ref.at[:, part_cols(c, a)], qbuf.at[a, c], qr.at[a * n + c]).start()
    for a in range(halves):
        pltpu.make_async_copy(g_ref.at[:, part_cols(c, a)], gbuf.at[a, c], gr.at[a * n + c]).start()

    for a in range(halves):
        @pl.loop(1, n)
        def _(s, a=a):
            p = partner(c, s, n)
            q_send(p, a).start()
            g_send(p, a).start()

    @pl.loop(0, n)
    def _(i):
        slab = kvbuf.at[d * n + i]
        pltpu.make_async_copy(slab, slab, kvr.at[i]).wait()

    @pl.loop(1, ndoc)
    def _(t):
        z_send(t).start()

    acc[...] = jnp.zeros_like(acc)
    gqp[...] = jnp.zeros_like(gqp)
    partp[...] = jnp.zeros_like(partp)
    finp[...] = jnp.zeros_like(finp)

    @pl.loop(1, ndoc)
    def _(t):
        slab = kvbuf.at[pl.ds(lax.rem(d - t + ndoc, ndoc) * n, n)]
        pltpu.make_async_copy(slab, slab, zr.at[t]).wait()

    both = kvbuf[...].astype(jnp.float32)
    keys[...] = both[:, :rows_p].reshape(total, width).astype(jnp.bfloat16)
    values[...] = both[:, rows_p:].reshape(total, width).astype(jnp.bfloat16)

    scale = HD ** (-0.5)

    def step(a, s, carry):
        p = source(c, s, n)
        pltpu.make_async_copy(qbuf.at[a, p], qbuf.at[a, p], qr.at[a * n + p]).wait()
        pltpu.make_async_copy(gbuf.at[a, p], gbuf.at[a, p], gr.at[a * n + p]).wait()
        for h in range(few):
            near = slice(h * HD, (h + 1) * HD)
            at = slice(a * part_w + h * HD, a * part_w + (h + 1) * HD)
            q, g = qbuf[a, p, :, near], gbuf[a, p, :, near]
            k, v = keys[:, at], values[:, at]
            expo = jnp.exp(dot(k, q, NT) * scale)
            if rows_p != rows:
                place = lax.broadcasted_iota(jnp.int32, expo.shape, 0)
                expo = jnp.where(lax.rem(place, rows_p) < rows, expo, 0.0)
            dprob = dot(v, g, NT)
            norm = jnp.sum(expo, axis=0, keepdims=True)
            drift = jnp.sum(expo * dprob, axis=0, keepdims=True) / norm
            prob = expo * (1.0 / norm)
            dscore = prob * (dprob - drift) * scale
            ds_hi, ds_lo = split16(dscore)
            pr_hi, pr_lo = split16(prob)
            grad_q = dot(ds_hi, k, TN) + dot(ds_lo, k, TN)
            peak = peak_of(grad_q, 0)
            gqp[p, a * few + h:a * few + h + 1] = peak
            gqbuf[a, p, :, near] = encode(grad_q, peak)
            grad_k = dot(ds_hi, q, NN) + dot(ds_lo, q, NN)
            grad_v = dot(pr_hi, g, NN) + dot(pr_lo, g, NN)
            acc[:, :rows_p, at] += grad_k.reshape(ndoc * n, rows_p, HD)
            acc[:, rows_p:, at] += grad_v.reshape(ndoc * n, rows_p, HD)

        @pl.when(s > 0)
        def _():
            o_send(p, a).start()
            if a == halves - 1:
                p_send(p).start()

        return carry

    for a in range(halves):
        lax.fori_loop(0, n, functools.partial(step, a), 0)
        chosen = slice(a * part_w, (a + 1) * part_w)
        tops = peaks_of(acc[:, :, chosen])
        for i, top in enumerate(tops):
            partp[a, i:i + 1] = top
        peaks = spread(partp[a], few)

        @pl.loop(1, ndoc)
        def _(t, a=a, chosen=chosen, peaks=peaks):
            to = pl.ds(lax.rem(d + t, ndoc) * n, n)
            part[a, to] = encode(acc[to, :, chosen], peaks[None])
            t_send(t, a).start()
            r_send(t, a).start()

        pltpu.make_async_copy(gqbuf.at[a, c], gq_out.at[:, part_cols(c, a)], orr.at[a * n + c]).start()

    gqp_own = pltpu.make_async_copy(gqp.at[c], gqp_out.at[c], pr.at[c])
    gqp_own.start()
    fin_src[...] = acc[pl.ds(d * n, n)]

    for a in range(halves):
        chosen = slice(a * part_w, (a + 1) * part_w)

        @pl.loop(1, ndoc)
        def _(t, a=a, chosen=chosen):
            t_send(t, a).wait_recv()
            r_send(t, a).wait_recv()
            fin_src[:, :, chosen] += decode(rsbuf[a, t], spread(rspbuf[a, t], few)[None])

    for i, top in enumerate(peaks_of(fin_src[...])):
        finp[i:i + 1] = top
    fin_enc[...] = encode(fin_src[...], spread(finp[...], nheads)[None])

    @pl.loop(1, n)
    def _(s):
        p = partner(c, s, n)
        u_send(p).start()
        f_send(p).start()

    fin[c] = fin_enc[c]
    fin_peaks[c] = finp[...]

    @pl.loop(1, n)
    def _(s):
        p = source(c, s, n)
        pltpu.make_async_copy(fin.at[p], fin.at[p], fr.at[p]).wait()
        pltpu.make_async_copy(fin_peaks.at[p], fin_peaks.at[p], ur.at[p]).wait()

    for i in range(n):
        at = slice(i * width, (i + 1) * width)
        gkv_out[:, at] = decode(fin[i], spread(fin_peaks[i], nheads))

    @pl.loop(0, n)
    def _(i):
        for a in range(halves):
            mine = gq_out.at[:, part_cols(i, a)]
            pltpu.make_async_copy(mine, mine, orr.at[a * n + i]).wait()
        peaks_in = gqp_out.at[i]
        pltpu.make_async_copy(peaks_in, peaks_in, pr.at[i]).wait()

    @pl.loop(1, n)
    def _(s):
        p = partner(c, s, n)
        kv_send(p).wait_send()
        for a in range(halves):
            q_send(p, a).wait_send()
            g_send(p, a).wait_send()
            o_send(p, a).wait_send()
        p_send(p).wait_send()
        f_send(p).wait_send()
        u_send(p).wait_send()

    @pl.loop(1, ndoc)
    def _(t):
        z_send(t).wait_send()
        for a in range(halves):
            r_send(t, a).wait_send()
            t_send(t, a).wait_send()


def up8(x):
    return -(-x // 8) * 8


def shards(queries, out_grad, mem_keys, mem_values):
    n, ndoc = lax.axis_size("ctx"), lax.axis_size("doc")
    qrows, features = queries.shape[1:]
    rows = mem_keys.shape[1]
    rows_p = up8(rows)
    width = features // n
    nheads = width // HD
    slabs = ndoc * n
    halves = max(i for i in (1, 2, 4) if nheads % i == 0)
    few = nheads // halves
    pad = ((0, rows_p - rows), (0, 0))
    kv = jnp.concatenate([jnp.pad(mem_keys[0], pad), jnp.pad(mem_values[0], pad)], axis=0)
    dma = pltpu.SemaphoreType.DMA
    vmem = pl.BlockSpec(memory_space=pltpu.VMEM)
    hbm = pl.BlockSpec(memory_space=pl.ANY)
    pairs = slabs * rows_p * n * qrows * width
    gq, gqp, gkv = pl.pallas_call(
        functools.partial(kernel, n, ndoc, rows, rows_p),
        out_shape=(
            jax.ShapeDtypeStruct((qrows, features), jnp.bfloat16),
            jax.ShapeDtypeStruct((n, up8(nheads), HD), jnp.float32),
            jax.ShapeDtypeStruct((2 * rows_p, features), jnp.float32),
        ),
        in_specs=[hbm, hbm, hbm],
        out_specs=(vmem, vmem, vmem),
        scratch_shapes=[
            pltpu.VMEM((halves, n, qrows, width // halves), jnp.bfloat16),
            pltpu.VMEM((halves, n, qrows, width // halves), jnp.bfloat16),
            pltpu.VMEM((slabs, 2 * rows_p, width), jnp.bfloat16),
            pltpu.VMEM((slabs * rows_p, width), jnp.bfloat16),
            pltpu.VMEM((slabs * rows_p, width), jnp.bfloat16),
            pltpu.VMEM((halves, n, qrows, width // halves), jnp.bfloat16),
            pltpu.VMEM((n, up8(nheads), HD), jnp.float32),
            pltpu.VMEM((slabs, 2 * rows_p, width), jnp.float32),
            pltpu.VMEM((halves, slabs, 2 * rows_p, width // halves), jnp.bfloat16),
            pltpu.VMEM((halves, up8(2 * few), HD), jnp.float32),
            pltpu.VMEM((halves, ndoc, n, 2 * rows_p, width // halves), jnp.bfloat16),
            pltpu.VMEM((halves, ndoc, up8(2 * few), HD), jnp.float32),
            pltpu.VMEM((n, 2 * rows_p, width), jnp.float32),
            pltpu.VMEM((n, 2 * rows_p, width), jnp.bfloat16),
            pltpu.VMEM((up8(2 * nheads), HD), jnp.float32),
            pltpu.VMEM((n, 2 * rows_p, width), jnp.bfloat16),
            pltpu.VMEM((n, up8(2 * nheads), HD), jnp.float32),
            dma((n,)), dma((n,)), *[dma((halves * n,))] * 4,
            dma((ndoc,)), dma((ndoc,)), dma((halves * n,)), dma((halves * n,)), dma((n,)), dma((n,)),
            *[dma((halves * ndoc,))] * 4, dma((n,)), dma((n,)), dma((n,)), dma((n,)),
        ],
        compiler_params=pltpu.CompilerParams(
            collective_id=0, has_side_effects=True, vmem_limit_bytes=58 * 1024 * 1024),
        cost_estimate=pl.CostEstimate(
            flops=16 * pairs, bytes_accessed=8 * qrows * features, transcendentals=pairs // HD),
    )(queries[0], out_grad[0], kv)
    gq = decode(gq, gqp[:, :nheads].reshape(1, features))
    return gq[None], gkv[None, :rows], gkv[None, rows_p:rows_p + rows]


def solution(mesh):
    placed = P("doc", "ctx", None)
    return jax.shard_map(
        shards,
        mesh=mesh,
        in_specs=(placed,) * 4,
        out_specs=(placed,) * 3,
        check_vma=False,
    )
```
